32 devices in a mesh: groups: 2 (over x), expert: 16 (over z, y, core).
Axes of the slice: x: 2, y: 2, z: 4, core: 2. Of those that a mesh axis runs over, the one named last changes fastest.
Arguments:
- tokens: bfloat16 [4096, 896], P(('groups', 'expert')), parts along dimension 0, may hold values from -6 to 6
- routes: int32 [4096, 2], P(('groups', 'expert')), parts along dimension 0, may hold values from 0 to 3, all different within a row; in each aligned block of 128 rows (0 to 127, 128 to 255, ...) at most 80 rows name the same one
- gate_weights: float32 [4096, 2], P(('groups', 'expert')), parts along dimension 0, may hold values from 0.2 to 1
- image_counts: int32 [32, 4], P(('groups', 'expert')), parts along dimension 0, may hold values from 1 to 64, 128 in all within a row
- cotangent: bfloat16 [4096, 896], P(('groups', 'expert')), parts along dimension 0, may hold values from -6 to 6
- up_weight: bfloat16 [16, 896, 1024], P('expert'), may hold values from -0.1875 to 0.1875
- down_weight: bfloat16 [16, 1024, 896], P('expert'), may hold values from -0.09375 to 0.09375
Outputs:
- layer_out: bfloat16 [4096, 896], P(('groups', 'expert')), parts along dimension 0
- token_grad: bfloat16 [4096, 896], P(('groups', 'expert')), parts along dimension 0
- up_grad: bfloat16 [32, 896, 1024], P(('groups', 'expert')), parts along dimension 0
- down_grad: bfloat16 [32, 1024, 896], P(('groups', 'expert')), parts along dimension 0
The draws below stay inside these ranges and needn't reach their ends.
There are 2 independent parts, one for each index of `groups`. The reference program is written for one: setup_inputs(seed, part) draws one part's arguments, and reference() takes and returns one part's arrays. A program takes and returns all parts, laid end to end along the dimension named above; an argument that names none is the same for every part. Nothing has to cross between parts.
Inputs may be any that keep to these rules, and one draw needn't show every extreme that they name: `routes`: in each device's 128 rows no expert is named by more than 80 rows, and in every draw some expert is named by exactly 80 of one device's rows; a row's two experts differ. `image_counts`: each row sums to 128 and its largest entry is 64.
All inputs are finite; a program needn't handle non-finite values.
Results may differ from the reference program's by a relative error of at most 0.0065.
Values may be sent and summed in bfloat16 or wider, within the bound.
A program may use at most 128 MiB of HBM per device.

```python
import math
import jax
import jax.numpy as jnp
import numpy as np
from jax import lax

D = 896
SPLIT = 4
HID_DEV = 1024
TOK_DEV = 128
IMG_DEV = 4
EXPERTS = 4
CAP = 80
TOKENS = 2048
N_EXPERT = 16


def block_scale(stream_key, extent, pieces, low, top_value):
    gain, own = 1.0, jax.random.fold_in(stream_key, 6)
    for dim, blocks in pieces:
        heights = jnp.exp(jax.random.uniform(jax.random.fold_in(own, dim), (blocks,), jnp.float32, low / len(pieces), top_value / len(pieces)))
        gain = gain * jnp.repeat(heights, extent[dim] // blocks).reshape([-1 if axis == dim else 1 for axis in range(len(extent))])
    return gain


def length_profile(count, total, limit, lean):
    weights = [(1 << 20) // math.isqrt(grade ** lean) + 1 for grade in range(2, count + 1)]
    surplus, holding = total - limit - (count - 1), [1] * (count - 1)
    while surplus > 0:
        free = [i for i in range(count - 1) if holding[i] < limit]
        whole, budget = sum([weights[i] for i in free]), surplus
        for i in free:
            more = min(limit - holding[i], max(1, budget * weights[i] // whole), surplus)
            holding[i] = holding[i] + more
            surplus = surplus - more
    return np.array([limit] + holding)


def ragged(rng, number_of, total, most, lean):
    if number_of == 2:
        one = jax.random.randint(rng, (), max(1, total - most), min(most, total - 1) + 1)
        return jnp.stack([one, total - one])
    lengths = jnp.asarray(length_profile(number_of, total, most, lean), jnp.int32)
    pairs = (number_of - 1) // 2
    giver, taker = lengths[1:1 + 2 * pairs:2], lengths[2:2 + 2 * pairs:2]
    room = jnp.minimum(giver - 1, most - taker)
    shifted = jax.random.randint(jax.random.fold_in(rng, 1), (pairs,), 0, 1 << 20) % (room + 1)
    lengths = lengths.at[1:1 + 2 * pairs:2].set(giver - shifted).at[2:2 + 2 * pairs:2].set(taker + shifted)
    return lengths[jax.random.permutation(jax.random.fold_in(rng, 2), number_of)]


def assign_block(own_key, own, number, rows, amount, top, most, slope):
    ranking = jax.random.permutation(own_key, amount)
    heavy_load, ordinary = load_shares(amount, rows * top, most, slope, True), load_shares(amount, rows * top, most, slope, False)
    places = jnp.arange(amount)

    def named(lengths, turn):
        used = int((lengths > 0).sum())
        fixed = max(1, used // 4)
        passed = fixed + (places - fixed + turn * (used - fixed)) % max(1, amount - fixed)
        return jnp.zeros((amount,), jnp.int32).at[ranking[jnp.where(places < fixed, places, passed)]].set(jnp.asarray(lengths, jnp.int32))

    lengths = jnp.where(number % 4 == 0, named(heavy_load, number // 4), named(ordinary, number - number // 4 - 1))
    mixed = jax.random.permutation(jax.random.fold_in(own, 3), amount)
    source_of, sink = mixed[0:amount // 2 * 2:2], mixed[1:amount // 2 * 2:2]
    room = jnp.minimum(lengths[source_of] - 1, most - lengths[sink]) // 2
    room = jnp.where((source_of == ranking[0]) | (sink == ranking[0]) | (lengths[sink] == 0), 0, jnp.maximum(room, 0))
    passed = jax.random.randint(jax.random.fold_in(own, 4), (amount // 2,), 0, 1 << 20) % (room + 1)
    lengths = lengths.at[source_of].add(-passed).at[sink].add(passed)
    members = jnp.searchsorted(jnp.cumsum(lengths), jnp.arange(rows * top), side="right").astype(jnp.int32)
    grid = members.reshape(top, rows).T
    grid = grid[jax.random.permutation(jax.random.fold_in(own, 1), rows)]
    turn = jax.random.randint(jax.random.fold_in(own, 2), (rows, 1), 0, top)
    return jnp.take_along_axis(grid, (jnp.arange(top)[None, :] + turn) % top, axis=1)


def load_shares(count, total, bound, lean, full):
    loads = [(1 << 20) // math.isqrt(standing ** lean) + 1 for standing in range(1, count + 1)]
    largest = bound if full else min(bound, max(-(-total // count), total * loads[0] // sum(loads)))
    least = 1 if total - largest >= count - 1 else 0
    counts, surplus = [largest] + [least] * (count - 1), total - largest - least * (count - 1)
    while surplus > 0:
        free = [i for i in range(1, count) if counts[i] < largest] or [i for i in range(1, count) if counts[i] < bound]
        mass, left = sum([loads[i] for i in free]), surplus
        for i in free:
            more = min(bound - counts[i], max(1, left * loads[i] // mass), surplus)
            counts[i] = counts[i] + more
            surplus = surplus - more
    return np.array(counts)


def scatter_about(own_key, shape, scale, bound, cuts=(), kind=jnp.bfloat16):
    result = jax.random.normal(own_key, shape, jnp.float32) * scale
    if len(cuts) > 0:
        result = block_scale(own_key, shape, cuts, -0.22, 0.18) * result
    return jnp.clip(result, min=-bound, max=bound).astype(kind)


def setup_inputs(seed: int = 0, part: int = 0) -> dict:
    seeds = jax.random.split(jax.random.key(seed), 8)
    part_keys = jax.random.split(jax.random.fold_in(seeds[7], part), 8)
    tokens = scatter_about(part_keys[0], (TOKENS, D), 1.0, 6.0, ((0, 16),))
    routes_keys = jax.random.split(jax.random.fold_in(part_keys[1], 1), TOKENS // TOK_DEV)
    routes_turns = jax.random.permutation(jax.random.fold_in(part_keys[1], 3), TOKENS // TOK_DEV)
    routes = jax.vmap(lambda own, number: assign_block(jax.random.fold_in(part_keys[1], 2), own, number, TOK_DEV, EXPERTS, 2, CAP, 2))(routes_keys, routes_turns).reshape((TOKENS, 2))
    gate_weights = jnp.clip(0.2 + 0.8 * jax.random.uniform(part_keys[2], (TOKENS, 2), jnp.float32) ** block_scale(part_keys[2], (TOKENS, 2), ((0, 16),), -0.2, 0.2), 0.2, 1.0)
    image_counts = jax.vmap(lambda own: ragged(own, IMG_DEV, TOK_DEV, TOK_DEV // 2, 2))(jax.random.split(part_keys[3], N_EXPERT)).reshape((N_EXPERT, IMG_DEV)).astype(jnp.int32)
    cotangent = scatter_about(part_keys[4], (TOKENS, D), 1.0, 6.0, ((0, 16),))
    up_weight = scatter_about(seeds[5], (N_EXPERT, D, HID_DEV), D ** -0.5, 0.1875, ((0, 16),))
    down_weight = scatter_about(seeds[6], (N_EXPERT, HID_DEV, D), (HID_DEV * SPLIT) ** -0.5, 0.09375, ((0, 16),))
    return dict(tokens=tokens, routes=routes, gate_weights=gate_weights, image_counts=image_counts, cotangent=cotangent, up_weight=up_weight, down_weight=down_weight)


def gelu_exact(value):
    return 0.5 * value * (1.0 + lax.erf(value * 0.7071067811865476))


def gelu_slope(value):
    return 0.5 * (1.0 + lax.erf(value * 0.7071067811865476)) + value * jnp.exp(-0.5 * value * value) * 0.3989422804014327


def slot_index(routes, capacity, experts):
    flat_routes = routes.reshape(-1)
    onehot = (flat_routes[:, None] == jnp.arange(experts, dtype=jnp.int32)[None, :]).astype(jnp.int32)
    before = jnp.cumsum(onehot, axis=0) - onehot
    rank = jnp.sum(before * onehot, axis=1)
    return (flat_routes * capacity + rank).astype(jnp.int32)


def fill_slots(slots, values, total):
    pair_ids = jnp.arange(slots.shape[0], dtype=jnp.int32)
    match = slots[None, :] == jnp.arange(total, dtype=jnp.int32)[:, None]
    source = jnp.sum(jnp.where(match, pair_ids[None, :], 0), axis=1).astype(jnp.int32)
    filled = jnp.any(match, axis=1)
    return jnp.where(filled[:, None], values[source], jnp.zeros((), values.dtype))


def token_scale(image_counts, tok_count):
    ends = jnp.cumsum(image_counts)
    position = jnp.arange(tok_count, dtype=jnp.int32)
    image = jnp.sum((position[:, None] >= ends[None, :]).astype(jnp.int32), axis=1)
    labels = jnp.arange(image_counts.shape[0], dtype=jnp.int32)
    own = jnp.sum(jnp.where(image[:, None] == labels[None, :], image_counts[None, :], 0), axis=1)
    return (tok_count / image_counts.shape[0]) / own.astype(jnp.float32)


def prepare_rows(tokens, routes, gate_weights, image_counts, cotangent, experts, capacity):
    tok_count = tokens.shape[0]
    width = tokens.shape[1]
    slots = slot_index(routes, capacity, experts)
    scale = token_scale(image_counts, tok_count)
    x_pairs = jnp.repeat(tokens, 2, axis=0)
    weighted = gate_weights * scale[:, None]
    dy_pairs = (weighted[:, :, None] * cotangent.astype(jnp.float32)[:, None, :]).reshape(2 * tok_count, width).astype(jnp.bfloat16)
    total = experts * capacity
    stacked = jnp.stack([fill_slots(slots, x_pairs, total), fill_slots(slots, dy_pairs, total)])
    return slots, stacked.reshape(2, experts, capacity, width)


def expert_quarter(rows_x, rows_dy, up_part, down_part):
    pre_act = jnp.dot(rows_x, up_part, preferred_element_type=jnp.float32)
    hidden = gelu_exact(pre_act).astype(jnp.bfloat16)
    out_part = jnp.dot(hidden, down_part, preferred_element_type=jnp.float32).astype(jnp.bfloat16)
    back_hidden = jnp.dot(rows_dy, down_part.T, preferred_element_type=jnp.float32)
    back_pre = (back_hidden * gelu_slope(pre_act)).astype(jnp.bfloat16)
    down_part_grad = jnp.dot(hidden.T, rows_dy, preferred_element_type=jnp.float32).astype(jnp.bfloat16)
    up_part_grad = jnp.dot(rows_x.T, back_pre, preferred_element_type=jnp.float32).astype(jnp.bfloat16)
    in_part = jnp.dot(back_pre, up_part.T, preferred_element_type=jnp.float32).astype(jnp.bfloat16)
    return out_part, in_part, up_part_grad, down_part_grad


def finish_rows(slots, sums, gate_weights):
    flat = sums.reshape(2, -1, sums.shape[-1])
    picked = flat[:, slots]
    tok_count = gate_weights.shape[0]
    outputs = picked[0].reshape(tok_count, 2, -1)
    layer_out = jnp.sum(gate_weights[:, :, None] * outputs, axis=1).astype(jnp.bfloat16)
    token_grad = jnp.sum(picked[1].reshape(tok_count, 2, -1), axis=1).astype(jnp.bfloat16)
    return layer_out, token_grad


def reference(tokens, routes, gate_weights, image_counts, cotangent, up_weight, down_weight):
    width = tokens.shape[1]

    def per_device(tok_block, route_block, gate_block, count_row, cot_block):
        return prepare_rows(tok_block, route_block, gate_block, count_row, cot_block, EXPERTS, CAP)

    slots, stacked = jax.vmap(per_device)(
        tokens.reshape(N_EXPERT, TOK_DEV, width),
        routes.reshape(N_EXPERT, TOK_DEV, 2),
        gate_weights.reshape(N_EXPERT, TOK_DEV, 2),
        image_counts,
        cotangent.reshape(N_EXPERT, TOK_DEV, width))
    up_all = up_weight.reshape(EXPERTS, SPLIT, width, HID_DEV)
    down_all = down_weight.reshape(EXPERTS, SPLIT, HID_DEV, width)

    def one_expert(expert):
        rows = stacked[:, :, expert]
        rows_x = rows[:, 0].reshape(-1, width)
        rows_dy = rows[:, 1].reshape(-1, width)
        out_sum = jnp.zeros((rows_x.shape[0], width), jnp.float32)
        in_sum = jnp.zeros((rows_x.shape[0], width), jnp.float32)
        up_list = []
        down_list = []
        for quarter in range(SPLIT):
            out_part, in_part, up_part_grad, down_part_grad = expert_quarter(rows_x, rows_dy, up_all[expert, quarter], down_all[expert, quarter])
            out_sum = out_sum + out_part.astype(jnp.float32)
            in_sum = in_sum + in_part.astype(jnp.float32)
            up_list.append(up_part_grad)
            down_list.append(down_part_grad)
        return out_sum, in_sum, jnp.stack(up_list), jnp.stack(down_list)

    out_sums, in_sums, up_grads, down_grads = lax.map(one_expert, jnp.arange(EXPERTS, dtype=jnp.int32))
    sums = jnp.stack([out_sums, in_sums], axis=1)
    sums = sums.reshape(EXPERTS, 2, N_EXPERT, CAP, width).transpose(2, 1, 0, 3, 4)
    layer_out, token_grad = jax.vmap(finish_rows)(slots, sums, gate_weights.reshape(N_EXPERT, TOK_DEV, 2))
    return (layer_out.reshape(-1, width), token_grad.reshape(-1, width),
            up_grads.reshape(N_EXPERT, width, HID_DEV), down_grads.reshape(N_EXPERT, HID_DEV, width))
```

```python
import functools

import jax
import jax.numpy as jnp
from jax import lax
from jax.experimental import pallas as pl
from jax.experimental.pallas import tpu as pltpu
from jax.sharding import PartitionSpec as P

SPLIT = 4
TILE = 256
Z, Y, C, F, R1, R2, R3 = range(7)


def kernel(
    experts, rt_ref, gt_ref, cnt_ref, tok_ref, cot_ref, u_hbm, v_hbm,
    lo_ref, tg_ref, ug_hbm, dg_hbm,
    u_ref, v_ref, send, rows, part, t1, t2, ret, hid, back, ug, dg,
    send_sem, recv_sem, w_sem, g_sem,
):
    me = lax.axis_index("expert")
    mine = me // SPLIT
    quarter = lax.rem(me, SPLIT)
    far = mine * SPLIT + lax.rem(quarter + 2, SPLIT)
    near = me + 1 - 2 * lax.rem(me, 2)
    tok, width = tok_ref.shape
    cap = send.shape[2]
    hidden = u_ref.shape[1]
    pieces = hidden // TILE
    bf, f32 = jnp.bfloat16, jnp.float32

    def dest(r):
        return lax.rem(mine - r + experts, experts)

    def source(r):
        return lax.rem(mine + r, experts)

    def copy(src, dst, kind, r, dev):
        return pltpu.make_async_remote_copy(
            src_ref=src, dst_ref=dst,
            send_sem=send_sem.at[kind, r], recv_sem=recv_sem.at[kind, r],
            device_id={"expert": dev}, device_id_type=pl.DeviceIdType.MESH,
        )

    def z_copy(r):
        return copy(send.at[r], rows.at[r, 0], Z, r, dest(r) * SPLIT + quarter)

    def y_copy(r):
        return copy(rows.at[r, 0], rows.at[r, 1], Y, r, far)

    def c_copy(r):
        return copy(rows.at[r, 0], rows.at[r, 2], C, r, near)

    def f_copy(r):
        return copy(rows.at[r, 1], rows.at[r, 3], F, r, near)

    def r1_copy(r):
        return copy(part.at[r, pl.ds(2, 2)], t1.at[r], R1, r, near)

    def r2_copy(r):
        return copy(part.at[r, 1], t2.at[r], R2, r, far)

    def r3_copy(r):
        return copy(part.at[r, 0], ret.at[r], R3, r, source(r) * SPLIT + quarter)

    u_copy = pltpu.make_async_copy(u_hbm.at[0], u_ref, w_sem.at[0])
    v_copy = pltpu.make_async_copy(v_hbm.at[0], v_ref, w_sem.at[1])
    u_copy.start()
    v_copy.start()

    barrier = pltpu.get_barrier_semaphore()
    for r in range(1, experts):
        pl.semaphore_signal(
            barrier, inc=1, device_id={"expert": dest(r) * SPLIT + quarter},
            device_id_type=pl.DeviceIdType.MESH,
        )
    for other in (far, near):
        pl.semaphore_signal(
            barrier, inc=1, device_id={"expert": other}, device_id_type=pl.DeviceIdType.MESH
        )

    heads = max(8, experts)
    row_id = lax.broadcasted_iota(jnp.int32, (heads, tok), 0)
    expert_id = lax.rem(mine - row_id + heads * experts, experts)
    r0 = jnp.broadcast_to(rt_ref[0:1, :], (heads, tok))
    r1 = jnp.broadcast_to(rt_ref[1:2, :], (heads, tok))
    g0 = jnp.broadcast_to(gt_ref[0:1, :], (heads, tok))
    g1 = jnp.broadcast_to(gt_ref[1:2, :], (heads, tok))
    takes0, takes1 = r0 == expert_id, r1 == expert_id
    member = jnp.where(takes0, 1.0, jnp.where(takes1, 1.0, 0.0))
    gate = jnp.where(takes0, g0, jnp.where(takes1, g1, 0.0))
    earlier = jnp.where(
        lax.broadcasted_iota(jnp.int32, (tok, tok), 0)
        < lax.broadcasted_iota(jnp.int32, (tok, tok), 1), 1.0, 0.0)
    rank = jnp.dot(member.astype(bf), earlier.astype(bf), preferred_element_type=f32)
    rank = jnp.where(member > 0.5, rank, -1.0)
    images = cnt_ref.shape[1]
    position = lax.broadcasted_iota(jnp.int32, (heads, tok), 1)
    own = jnp.ones((heads, tok), jnp.int32)
    start = jnp.int32(0)
    for j in range(images):
        count = cnt_ref[0, j]
        own = jnp.where(position >= start, count, own)
        start = start + count
    weight = gate * ((tok / images) / own.astype(f32))
    gate_col = jnp.transpose(gate)
    slot_id = lax.broadcasted_iota(jnp.int32, (cap, tok), 0).astype(f32)

    def choose(r):
        return slot_id == jnp.broadcast_to(rank[r:r + 1], (cap, tok))

    def fill(r, dst):
        hit = choose(r)
        pick = jnp.where(hit, 1.0, 0.0).astype(bf)
        w = jnp.sum(
            jnp.where(hit, jnp.broadcast_to(weight[r:r + 1], (cap, tok)), 0.0),
            axis=1, keepdims=True)
        dst[0] = jnp.dot(pick, tok_ref[...], preferred_element_type=f32).astype(bf)
        dst[1] = (jnp.dot(pick, cot_ref[...], preferred_element_type=f32) * w).astype(bf)

    fill(0, rows.at[0, 0])
    pl.semaphore_wait(barrier, experts + 1)
    y_copy(0).start()
    c_copy(0).start()
    for r in range(1, experts):
        fill(r, send.at[r])
        z_copy(r).start()
    u_copy.wait()
    v_copy.wait()

    def pair_sum(r):
        r1_copy(r).wait_recv()
        for j in (1, 0):
            part[r, j] = (part[r, j].astype(f32) + t1[r, j].astype(f32)).astype(bf)
            if j == 1:
                r2_copy(r).start()

    def step(r, carry):
        @pl.when(r + 1 < experts)
        def _():
            z_copy(r + 1).wait_recv()
            y_copy(r + 1).start()
            c_copy(r + 1).start()

        y_copy(r).wait_recv()
        f_copy(r).start()
        c_copy(r).wait_recv()
        f_copy(r).wait_recv()

        def tile(n, carry):
            col = pl.ds(pl.multiple_of(n * TILE, TILE), TILE)
            x = rows[r, :, 0].reshape(SPLIT * cap, width)
            g = rows[r, :, 1].reshape(SPLIT * cap, width)
            pre = jnp.dot(x, u_ref[:, col], preferred_element_type=f32)
            gv = lax.dot_general(
                g, v_ref[col, :], (((1,), (1,)), ((), ())), preferred_element_type=f32)
            phi = 0.5 * (1.0 + lax.erf(pre * 0.7071067811865476))
            hid[r, :, col] = (pre * phi).astype(bf)
            slope = phi + pre * jnp.exp(-0.5 * pre * pre) * 0.3989422804014327
            back[r, :, col] = (gv * slope).astype(bf)
            return carry

        lax.fori_loop(0, pieces, tile, 0)
        out = jnp.dot(hid[r], v_ref[...], preferred_element_type=f32)
        part[r, :, 0] = out.astype(bf).reshape(SPLIT, cap, width)
        inn = lax.dot_general(
            back[r], u_ref[...], (((1,), (1,)), ((), ())), preferred_element_type=f32)
        part[r, :, 1] = inn.astype(bf).reshape(SPLIT, cap, width)
        r1_copy(r).start()

        @pl.when(r >= 1)
        def _():
            pair_sum(r - 1)

        return carry

    lax.fori_loop(0, experts, step, 0)
    pair_sum(experts - 1)

    def quad_sum(r):
        r2_copy(r).wait_recv()
        part[r, 0] = (part[r, 0].astype(f32) + t2[r].astype(f32)).astype(bf)

        @pl.when(r >= 1)
        def _():
            r3_copy(r).start()

    def ug_copy(n):
        col = pl.ds(pl.multiple_of(n * TILE, TILE), TILE)
        return pltpu.make_async_copy(ug.at[:, col], ug_hbm.at[0, :, col], g_sem.at[0, n])

    def dg_copy(n):
        col = pl.ds(pl.multiple_of(n * TILE, TILE), TILE)
        return pltpu.make_async_copy(dg.at[col, :], dg_hbm.at[0, col, :], g_sem.at[1, n])

    total = experts * SPLIT * cap
    per = -(-experts // pieces)

    def grads(n, carry):
        for j in range(per):
            r = n * per + j

            @pl.when(r < experts)
            def _():
                quad_sum(r)

        col = pl.ds(pl.multiple_of(n * TILE, TILE), TILE)
        x = rows[:, :, 0].reshape(total, width)
        b = back[:, :, col].reshape(total, TILE)
        ug[:, col] = lax.dot_general(
            x, b, (((0,), (0,)), ((), ())), preferred_element_type=f32).astype(bf)
        ug_copy(n).start()
        g = rows[:, :, 1].reshape(total, width)
        h = hid[:, :, col].reshape(total, TILE)
        dg[col, :] = lax.dot_general(
            h, g, (((0,), (0,)), ((), ())), preferred_element_type=f32).astype(bf)
        dg_copy(n).start()
        return carry

    lax.fori_loop(0, pieces, grads, 0)

    layer = jnp.zeros((tok, width), f32)
    grad = jnp.zeros((tok, width), f32)
    for r in range(experts):
        if r:
            r3_copy(r).wait_recv()
        block = ret.at[r] if r else part.at[0, 0]
        pick = jnp.where(choose(r), 1.0, 0.0).astype(bf)
        picked = lax.dot_general(
            pick, block[0], (((0,), (0,)), ((), ())), preferred_element_type=f32)
        layer = layer + picked * gate_col[:, r:r + 1]
        grad = grad + lax.dot_general(
            pick, block[1], (((0,), (0,)), ((), ())), preferred_element_type=f32)
    lo_ref[...] = layer.astype(bf)
    tg_ref[...] = grad.astype(bf)

    def drain(r, carry):
        y_copy(r).wait_send()
        c_copy(r).wait_send()
        f_copy(r).wait_send()
        r1_copy(r).wait_send()
        r2_copy(r).wait_send()

        @pl.when(r >= 1)
        def _():
            z_copy(r).wait_send()
            r3_copy(r).wait_send()

        return carry

    lax.fori_loop(0, experts, drain, 0)

    def drain_grads(n, carry):
        ug_copy(n).wait()
        dg_copy(n).wait()
        return carry

    lax.fori_loop(0, pieces, drain_grads, 0)


def local(tokens, routes, gate_weights, image_counts, cotangent, up_weight, down_weight):
    shards = lax.axis_size("expert")
    experts = shards // SPLIT
    tok, width = tokens.shape
    hidden = up_weight.shape[2]
    capacity = SPLIT * ((10 * tok + 4 * SPLIT * experts - 1) // (4 * SPLIT * experts))
    cap = -(-capacity // 16) * 16
    bf = jnp.bfloat16
    vmem = pl.BlockSpec(memory_space=pltpu.VMEM)
    smem = pl.BlockSpec(memory_space=pltpu.SMEM)
    hbm = pl.BlockSpec(memory_space=pl.ANY)
    rows = experts * SPLIT * cap
    return pl.pallas_call(
        functools.partial(kernel, experts),
        out_shape=(
            jax.ShapeDtypeStruct((tok, width), bf),
            jax.ShapeDtypeStruct((tok, width), bf),
            jax.ShapeDtypeStruct((1, width, hidden), bf),
            jax.ShapeDtypeStruct((1, hidden, width), bf),
        ),
        in_specs=[vmem, vmem, smem, vmem, vmem, hbm, hbm],
        out_specs=(vmem, vmem, hbm, hbm),
        scratch_shapes=[
            pltpu.VMEM((width, hidden), bf),
            pltpu.VMEM((hidden, width), bf),
            pltpu.VMEM((experts, 2, cap, width), bf),
            pltpu.VMEM((experts, SPLIT, 2, cap, width), bf),
            pltpu.VMEM((experts, SPLIT, 2, cap, width), bf),
            pltpu.VMEM((experts, 2, 2, cap, width), bf),
            pltpu.VMEM((experts, 2, cap, width), bf),
            pltpu.VMEM((experts, 2, cap, width), bf),
            pltpu.VMEM((experts, SPLIT * cap, hidden), bf),
            pltpu.VMEM((experts, SPLIT * cap, hidden), bf),
            pltpu.VMEM((width, hidden), bf),
            pltpu.VMEM((hidden, width), bf),
            pltpu.SemaphoreType.DMA((7, experts)),
            pltpu.SemaphoreType.DMA((7, experts)),
            pltpu.SemaphoreType.DMA((2,)),
            pltpu.SemaphoreType.DMA((2, hidden // TILE)),
        ],
        compiler_params=pltpu.CompilerParams(
            collective_id=0, has_side_effects=True, vmem_limit_bytes=58 * 1024 * 1024
        ),
        cost_estimate=pl.CostEstimate(
            flops=12 * rows * width * hidden,
            bytes_accessed=8 * width * hidden,
            transcendentals=2 * rows * hidden,
        ),
    )(routes.T, gate_weights.T, image_counts, tokens, cotangent, up_weight, down_weight)


def solution(mesh):
    placed = (
        P(("groups", "expert"), None),
        P(("groups", "expert"), None),
        P(("groups", "expert"), None),
        P(("groups", "expert"), None),
        P(("groups", "expert"), None),
        P("expert", None, None),
        P("expert", None, None),
    )
    return jax.shard_map(
        local,
        mesh=mesh,
        in_specs=placed,
        out_specs=(
            P(("groups", "expert"), None),
            P(("groups", "expert"), None),
            P(("groups", "expert"), None, None),
            P(("groups", "expert"), None, None),
        ),
        check_vma=False,
    )
```

```python
import functools

import jax
import jax.numpy as jnp
from jax import lax
from jax.experimental import pallas as pl
from jax.experimental.pallas import tpu as pltpu
from jax.sharding import PartitionSpec as P

SPLIT = 4
TILE = 256
Z, Y, C, F, R1, R2, R3 = range(7)


def kernel(
    experts, rt_ref, gt_ref, cnt_ref, tok_ref, cot_ref, u_hbm, v_hbm,
    lo_ref, tg_ref, ug_hbm, dg_hbm,
    u_ref, v_ref, send, rows, part, t1, t2, ret, hid, back, ug, dg,
    send_sem, recv_sem, w_sem, g_sem,
):
    me = lax.axis_index("expert")
    mine = me // SPLIT
    quarter = lax.rem(me, SPLIT)
    far = mine * SPLIT + lax.rem(quarter + 2, SPLIT)
    near = me + 1 - 2 * lax.rem(me, 2)
    tok, width = tok_ref.shape
    cap = send.shape[2]
    hidden = u_ref.shape[1]
    pieces = hidden // TILE
    bf, f32 = jnp.bfloat16, jnp.float32

    def turn(r):
        half = (r + 1) // 2
        return half if r % 2 else experts - half

    def turn_of(r):
        if isinstance(r, int):
            return turn(r)
        half = (r + 1) // 2
        return jnp.where(lax.rem(r, 2) == 1, half, experts - half)

    def dest(r):
        return lax.rem(mine - turn_of(r) + experts, experts)

    def source(r):
        return lax.rem(mine + turn_of(r), experts)

    def copy(src, dst, kind, r, dev):
        return pltpu.make_async_remote_copy(
            src_ref=src, dst_ref=dst,
            send_sem=send_sem.at[kind, r], recv_sem=recv_sem.at[kind, r],
            device_id={"expert": dev}, device_id_type=pl.DeviceIdType.MESH,
        )

    def z_copy(r):
        return copy(send.at[r], rows.at[r, 0], Z, r, dest(r) * SPLIT + quarter)

    def y_copy(r):
        return copy(rows.at[r, 0], rows.at[r, 1], Y, r, far)

    def c_copy(r):
        return copy(rows.at[r, 0], rows.at[r, 2], C, r, near)

    def f_copy(r):
        return copy(rows.at[r, 1], rows.at[r, 3], F, r, near)

    def r1_copy(r):
        return copy(part.at[r, pl.ds(2, 2)], t1.at[r], R1, r, near)

    def r2_copy(r):
        return copy(part.at[r, 1], t2.at[r], R2, r, far)

    def r3_copy(r):
        return copy(part.at[r, 0], ret.at[r], R3, r, source(r) * SPLIT + quarter)

    u_copy = pltpu.make_async_copy(u_hbm.at[0], u_ref, w_sem.at[0])
    v_copy = pltpu.make_async_copy(v_hbm.at[0], v_ref, w_sem.at[1])
    u_copy.start()
    v_copy.start()

    barrier = pltpu.get_barrier_semaphore()
    for r in range(1, experts):
        pl.semaphore_signal(
            barrier, inc=1, device_id={"expert": dest(r) * SPLIT + quarter},
            device_id_type=pl.DeviceIdType.MESH,
        )
    for other in (far, near):
        pl.semaphore_signal(
            barrier, inc=1, device_id={"expert": other}, device_id_type=pl.DeviceIdType.MESH
        )

    heads = max(8, experts)
    row_id = lax.broadcasted_iota(jnp.int32, (heads, tok), 0)
    expert_id = lax.rem(mine - turn_of(row_id) + heads * experts, experts)
    r0 = jnp.broadcast_to(rt_ref[0:1, :], (heads, tok))
    r1 = jnp.broadcast_to(rt_ref[1:2, :], (heads, tok))
    g0 = jnp.broadcast_to(gt_ref[0:1, :], (heads, tok))
    g1 = jnp.broadcast_to(gt_ref[1:2, :], (heads, tok))
    takes0, takes1 = r0 == expert_id, r1 == expert_id
    member = jnp.where(takes0, 1.0, jnp.where(takes1, 1.0, 0.0))
    gate = jnp.where(takes0, g0, jnp.where(takes1, g1, 0.0))
    earlier = jnp.where(
        lax.broadcasted_iota(jnp.int32, (tok, tok), 0)
        < lax.broadcasted_iota(jnp.int32, (tok, tok), 1), 1.0, 0.0)
    rank = jnp.dot(member.astype(bf), earlier.astype(bf), preferred_element_type=f32)
    rank = jnp.where(member > 0.5, rank, -1.0)
    images = cnt_ref.shape[1]
    position = lax.broadcasted_iota(jnp.int32, (heads, tok), 1)
    own = jnp.ones((heads, tok), jnp.int32)
    start = jnp.int32(0)
    for j in range(images):
        count = cnt_ref[0, j]
        own = jnp.where(position >= start, count, own)
        start = start + count
    weight = gate * ((tok / images) / own.astype(f32))
    gate_col = jnp.transpose(gate)
    slot_id = lax.broadcasted_iota(jnp.int32, (cap, tok), 0).astype(f32)

    def choose(r):
        return slot_id == jnp.broadcast_to(rank[r:r + 1], (cap, tok))

    def fill(r, dst):
        hit = choose(r)
        pick = jnp.where(hit, 1.0, 0.0).astype(bf)
        w = jnp.sum(
            jnp.where(hit, jnp.broadcast_to(weight[r:r + 1], (cap, tok)), 0.0),
            axis=1, keepdims=True)
        dst[0] = jnp.dot(pick, tok_ref[...], preferred_element_type=f32).astype(bf)
        dst[1] = (jnp.dot(pick, cot_ref[...], preferred_element_type=f32) * w).astype(bf)

    fill(0, rows.at[0, 0])
    pl.semaphore_wait(barrier, experts + 1)
    y_copy(0).start()
    c_copy(0).start()
    for r in range(1, experts):
        fill(r, send.at[r])
        if r == 1:
            z_copy(1).start()
    z_copy(1).wait_send()
    z_copy(2).start()
    u_copy.wait()
    v_copy.wait()

    def pair_sum(r):
        r1_copy(r).wait_recv()
        for j in (1, 0):
            part[r, j] = (part[r, j].astype(f32) + t1[r, j].astype(f32)).astype(bf)
            if j == 1:
                r2_copy(r).start()

    def quad_sum(r):
        r2_copy(r).wait_recv()
        part[r, 0] = (part[r, 0].astype(f32) + t2[r].astype(f32)).astype(bf)

        @pl.when(jnp.int32(r) >= 1)
        def _():
            r3_copy(r).start()

    def step(r, carry):
        @pl.when(r + 1 < experts)
        def _():
            z_copy(r + 1).wait_recv()
            y_copy(r + 1).start()
            c_copy(r + 1).start()

        y_copy(r).wait_recv()
        f_copy(r).start()

        @pl.when(r >= 1)
        def _():
            pair_sum(r - 1)

        @pl.when(r >= 2)
        def _():
            quad_sum(r - 2)

        c_copy(r).wait_recv()
        f_copy(r).wait_recv()

        def tile(n, carry):
            col = pl.ds(pl.multiple_of(n * TILE, TILE), TILE)
            x = rows[r, :, 0].reshape(SPLIT * cap, width)
            g = rows[r, :, 1].reshape(SPLIT * cap, width)
            pre = jnp.dot(x, u_ref[:, col], preferred_element_type=f32)
            gv = lax.dot_general(
                g, v_ref[col, :], (((1,), (1,)), ((), ())), preferred_element_type=f32)
            phi = 0.5 * (1.0 + lax.erf(pre * 0.7071067811865476))
            hid[r, :, col] = (pre * phi).astype(bf)
            slope = phi + pre * jnp.exp(-0.5 * pre * pre) * 0.3989422804014327
            back[r, :, col] = (gv * slope).astype(bf)
            return carry

        lax.fori_loop(0, pieces, tile, 0)

        @pl.when(r + 3 < experts)
        def _():
            z_copy(r + 2).wait_send()
            z_copy(r + 3).start()

        out = jnp.dot(hid[r], v_ref[...], preferred_element_type=f32)
        part[r, :, 0] = out.astype(bf).reshape(SPLIT, cap, width)
        inn = lax.dot_general(
            back[r], u_ref[...], (((1,), (1,)), ((), ())), preferred_element_type=f32)
        part[r, :, 1] = inn.astype(bf).reshape(SPLIT, cap, width)
        r1_copy(r).start()
        return carry

    lax.fori_loop(0, experts, step, 0)
    def ug_copy(n):
        col = pl.ds(pl.multiple_of(n * TILE, TILE), TILE)
        return pltpu.make_async_copy(ug.at[:, col], ug_hbm.at[0, :, col], g_sem.at[0, n])

    def dg_copy(n):
        col = pl.ds(pl.multiple_of(n * TILE, TILE), TILE)
        return pltpu.make_async_copy(dg.at[col, :], dg_hbm.at[0, col, :], g_sem.at[1, n])

    total = experts * SPLIT * cap

    def grads(n, carry):
        @pl.when(n == 1)
        def _():
            pair_sum(experts - 1)
            quad_sum(experts - 2)

        @pl.when(n == pieces - 1)
        def _():
            quad_sum(experts - 1)

        col = pl.ds(pl.multiple_of(n * TILE, TILE), TILE)
        x = rows[:, :, 0].reshape(total, width)
        b = back[:, :, col].reshape(total, TILE)
        ug[:, col] = lax.dot_general(
            x, b, (((0,), (0,)), ((), ())), preferred_element_type=f32).astype(bf)
        ug_copy(n).start()
        g = rows[:, :, 1].reshape(total, width)
        h = hid[:, :, col].reshape(total, TILE)
        dg[col, :] = lax.dot_general(
            h, g, (((0,), (0,)), ((), ())), preferred_element_type=f32).astype(bf)
        dg_copy(n).start()
        return carry

    lax.fori_loop(0, pieces, grads, 0)

    layer = jnp.zeros((tok, width), f32)
    grad = jnp.zeros((tok, width), f32)
    for r in range(experts):
        if r:
            r3_copy(r).wait_recv()
        block = ret.at[r] if r else part.at[0, 0]
        pick = jnp.where(choose(r), 1.0, 0.0).astype(bf)
        picked = lax.dot_general(
            pick, block[0], (((0,), (0,)), ((), ())), preferred_element_type=f32)
        layer = layer + picked * gate_col[:, r:r + 1]
        grad = grad + lax.dot_general(
            pick, block[1], (((0,), (0,)), ((), ())), preferred_element_type=f32)
    lo_ref[...] = layer.astype(bf)
    tg_ref[...] = grad.astype(bf)

    def drain(r, carry):
        y_copy(r).wait_send()
        c_copy(r).wait_send()
        f_copy(r).wait_send()
        r1_copy(r).wait_send()
        r2_copy(r).wait_send()

        @pl.when(r >= 1)
        def _():
            r3_copy(r).wait_send()

        return carry

    lax.fori_loop(0, experts, drain, 0)
    z_copy(experts - 1).wait_send()

    def drain_grads(n, carry):
        ug_copy(n).wait()
        dg_copy(n).wait()
        return carry

    lax.fori_loop(0, pieces, drain_grads, 0)


def local(tokens, routes, gate_weights, image_counts, cotangent, up_weight, down_weight):
    shards = lax.axis_size("expert")
    experts = shards // SPLIT
    tok, width = tokens.shape
    hidden = up_weight.shape[2]
    capacity = SPLIT * ((10 * tok + 4 * SPLIT * experts - 1) // (4 * SPLIT * experts))
    cap = -(-capacity // 16) * 16
    bf = jnp.bfloat16
    vmem = pl.BlockSpec(memory_space=pltpu.VMEM)
    smem = pl.BlockSpec(memory_space=pltpu.SMEM)
    hbm = pl.BlockSpec(memory_space=pl.ANY)
    rows = experts * SPLIT * cap
    return pl.pallas_call(
        functools.partial(kernel, experts),
        out_shape=(
            jax.ShapeDtypeStruct((tok, width), bf),
            jax.ShapeDtypeStruct((tok, width), bf),
            jax.ShapeDtypeStruct((1, width, hidden), bf),
            jax.ShapeDtypeStruct((1, hidden, width), bf),
        ),
        in_specs=[vmem, vmem, smem, vmem, vmem, hbm, hbm],
        out_specs=(vmem, vmem, hbm, hbm),
        scratch_shapes=[
            pltpu.VMEM((width, hidden), bf),
            pltpu.VMEM((hidden, width), bf),
            pltpu.VMEM((experts, 2, cap, width), bf),
            pltpu.VMEM((experts, SPLIT, 2, cap, width), bf),
            pltpu.VMEM((experts, SPLIT, 2, cap, width), bf),
            pltpu.VMEM((experts, 2, 2, cap, width), bf),
            pltpu.VMEM((experts, 2, cap, width), bf),
            pltpu.VMEM((experts, 2, cap, width), bf),
            pltpu.VMEM((experts, SPLIT * cap, hidden), bf),
            pltpu.VMEM((experts, SPLIT * cap, hidden), bf),
            pltpu.VMEM((width, hidden), bf),
            pltpu.VMEM((hidden, width), bf),
            pltpu.SemaphoreType.DMA((7, experts)),
            pltpu.SemaphoreType.DMA((7, experts)),
            pltpu.SemaphoreType.DMA((2,)),
            pltpu.SemaphoreType.DMA((2, hidden // TILE)),
        ],
        compiler_params=pltpu.CompilerParams(
            collective_id=0, has_side_effects=True, vmem_limit_bytes=58 * 1024 * 1024
        ),
        cost_estimate=pl.CostEstimate(
            flops=12 * rows * width * hidden,
            bytes_accessed=8 * width * hidden,
            transcendentals=2 * rows * hidden,
        ),
    )(routes.T, gate_weights.T, image_counts, tokens, cotangent, up_weight, down_weight)


def solution(mesh):
    placed = (
        P(("groups", "expert"), None),
        P(("groups", "expert"), None),
        P(("groups", "expert"), None),
        P(("groups", "expert"), None),
        P(("groups", "expert"), None),
        P("expert", None, None),
        P("expert", None, None),
    )
    return jax.shard_map(
        local,
        mesh=mesh,
        in_specs=placed,
        out_specs=(
            P(("groups", "expert"), None),
            P(("groups", "expert"), None),
            P(("groups", "expert"), None, None),
            P(("groups", "expert"), None, None),
        ),
        check_vma=False,
    )
```

```python
import functools

import jax
import jax.numpy as jnp
from jax import lax
from jax.experimental import pallas as pl
from jax.experimental.pallas import tpu as pltpu
from jax.sharding import PartitionSpec as P

SPLIT = 4
TILE = 256
Z, Y, C, F, R1, R2, R3 = range(7)


def kernel(
    experts, rt_ref, gt_ref, cnt_ref, tok_ref, cot_ref, u_hbm, v_hbm,
    lo_ref, tg_ref, ug_hbm, dg_hbm,
    u_ref, v_ref, send, rows, part, t1, t2, ret, hid, back, ug, dg,
    send_sem, recv_sem, w_sem, g_sem,
):
    me = lax.axis_index("expert")
    mine = me // SPLIT
    quarter = lax.rem(me, SPLIT)
    far = mine * SPLIT + lax.rem(quarter + 2, SPLIT)
    near = me + 1 - 2 * lax.rem(me, 2)
    tok, width = tok_ref.shape
    cap = send.shape[2]
    hidden = u_ref.shape[1]
    pieces = hidden // TILE
    bf, f32 = jnp.bfloat16, jnp.float32

    def turn(r):
        half = (r + 1) // 2
        return half if r % 2 else experts - half

    def turn_of(r):
        if isinstance(r, int):
            return turn(r)
        half = (r + 1) // 2
        return jnp.where(lax.rem(r, 2) == 1, half, experts - half)

    def dest(r):
        return lax.rem(mine - turn_of(r) + experts, experts)

    def source(r):
        return lax.rem(mine + turn_of(r), experts)

    def copy(src, dst, kind, r, h, dev):
        return pltpu.make_async_remote_copy(
            src_ref=src, dst_ref=dst,
            send_sem=send_sem.at[kind, r, h], recv_sem=recv_sem.at[kind, r, h],
            device_id={"expert": dev}, device_id_type=pl.DeviceIdType.MESH,
        )

    def z_copy(r, h):
        return copy(send.at[r, h], rows.at[r, 0, h], Z, r, h, dest(r) * SPLIT + quarter)

    def y_copy(r, h):
        return copy(rows.at[r, 0, h], rows.at[r, 1, h], Y, r, h, far)

    def c_copy(r, h):
        return copy(rows.at[r, 0, h], rows.at[r, 2, h], C, r, h, near)

    def f_copy(r, h):
        return copy(rows.at[r, 1, h], rows.at[r, 3, h], F, r, h, near)

    def r1_copy(r, h):
        return copy(part.at[r, pl.ds(2, 2), h], t1.at[r, :, h], R1, r, h, near)

    def r2_copy(r, h):
        return copy(part.at[r, 1, h], t2.at[r, h], R2, r, h, far)

    def r3_copy(r, h):
        return copy(part.at[r, 0, h], ret.at[r, h], R3, r, h, source(r) * SPLIT + quarter)

    u_copy = pltpu.make_async_copy(u_hbm.at[0], u_ref, w_sem.at[0])
    v_copy = pltpu.make_async_copy(v_hbm.at[0], v_ref, w_sem.at[1])
    u_copy.start()
    v_copy.start()

    barrier = pltpu.get_barrier_semaphore()
    for r in range(1, experts):
        pl.semaphore_signal(
            barrier, inc=1, device_id={"expert": dest(r) * SPLIT + quarter},
            device_id_type=pl.DeviceIdType.MESH,
        )
    for other in (far, near):
        pl.semaphore_signal(
            barrier, inc=1, device_id={"expert": other}, device_id_type=pl.DeviceIdType.MESH
        )

    heads = max(8, experts)
    row_id = lax.broadcasted_iota(jnp.int32, (heads, tok), 0)
    expert_id = lax.rem(mine - turn_of(row_id) + heads * experts, experts)
    r0 = jnp.broadcast_to(rt_ref[0:1, :], (heads, tok))
    r1 = jnp.broadcast_to(rt_ref[1:2, :], (heads, tok))
    g0 = jnp.broadcast_to(gt_ref[0:1, :], (heads, tok))
    g1 = jnp.broadcast_to(gt_ref[1:2, :], (heads, tok))
    takes0, takes1 = r0 == expert_id, r1 == expert_id
    member = jnp.where(takes0, 1.0, jnp.where(takes1, 1.0, 0.0))
    gate = jnp.where(takes0, g0, jnp.where(takes1, g1, 0.0))
    earlier = jnp.where(
        lax.broadcasted_iota(jnp.int32, (tok, tok), 0)
        < lax.broadcasted_iota(jnp.int32, (tok, tok), 1), 1.0, 0.0)
    rank = jnp.dot(member.astype(bf), earlier.astype(bf), preferred_element_type=f32)
    rank = jnp.where(member > 0.5, rank, -1.0)
    images = cnt_ref.shape[1]
    position = lax.broadcasted_iota(jnp.int32, (heads, tok), 1)
    own = jnp.ones((heads, tok), jnp.int32)
    start = jnp.int32(0)
    for j in range(images):
        count = cnt_ref[0, j]
        own = jnp.where(position >= start, count, own)
        start = start + count
    weight = gate * ((tok / images) / own.astype(f32))
    gate_col = jnp.transpose(gate)
    slot_id = lax.broadcasted_iota(jnp.int32, (cap, tok), 0).astype(f32)

    def choose(r):
        return slot_id == jnp.broadcast_to(rank[r:r + 1], (cap, tok))

    def fill(r, dst, send_half):
        hit = choose(r)
        pick = jnp.where(hit, 1.0, 0.0).astype(bf)
        dst[0] = jnp.dot(pick, tok_ref[...], preferred_element_type=f32).astype(bf)
        send_half(0)
        w = jnp.sum(
            jnp.where(hit, jnp.broadcast_to(weight[r:r + 1], (cap, tok)), 0.0),
            axis=1, keepdims=True)
        dst[1] = (jnp.dot(pick, cot_ref[...], preferred_element_type=f32) * w).astype(bf)
        send_half(1)

    def send_own(h):
        y_copy(0, h).start()
        c_copy(0, h).start()

    def send_first(h):
        z_copy(1, h).start()

    pl.semaphore_wait(barrier, experts + 1)
    fill(1, send.at[1], send_first)
    fill(0, rows.at[0, 0], send_own)
    for r in range(2, experts):
        fill(r, send.at[r], lambda h: None)
    for h in range(2):
        z_copy(1, h).wait_send()
        z_copy(2, h).start()
    u_copy.wait()
    v_copy.wait()

    def pair_sum(r):
        for h in range(2):
            r1_copy(r, h).wait_recv()
            for j in (1, 0):
                part[r, j, h] = (part[r, j, h].astype(f32) + t1[r, j, h].astype(f32)).astype(bf)
                if j == 1:
                    r2_copy(r, h).start()

    def quad_sum(r, h):
        r2_copy(r, h).wait_recv()
        part[r, 0, h] = (part[r, 0, h].astype(f32) + t2[r, h].astype(f32)).astype(bf)

        @pl.when(jnp.int32(r) >= 1)
        def _():
            r3_copy(r, h).start()

    def step(r, carry):
        for h in range(2):
            y_copy(r, h).wait_recv()
            f_copy(r, h).start()

        @pl.when(r >= 2)
        def _():
            pair_sum(r - 1)

        @pl.when(r + 1 < experts)
        def _():
            for h in range(2):
                z_copy(r + 1, h).wait_recv()
                y_copy(r + 1, h).start()
                c_copy(r + 1, h).start()

        @pl.when(r == 1)
        def _():
            pair_sum(0)

        @pl.when(r >= 2)
        def _():
            for h in range(2):
                quad_sum(r - 2, h)

        for h in range(2):
            c_copy(r, h).wait_recv()
            f_copy(r, h).wait_recv()

        def tile(n, carry):
            col = pl.ds(pl.multiple_of(n * TILE, TILE), TILE)
            x = rows[r, :, 0].reshape(SPLIT * cap, width)
            g = rows[r, :, 1].reshape(SPLIT * cap, width)
            pre = jnp.dot(x, u_ref[:, col], preferred_element_type=f32)
            gv = lax.dot_general(
                g, v_ref[col, :], (((1,), (1,)), ((), ())), preferred_element_type=f32)
            phi = 0.5 * (1.0 + lax.erf(pre * 0.7071067811865476))
            hid[r, :, col] = (pre * phi).astype(bf)
            slope = phi + pre * jnp.exp(-0.5 * pre * pre) * 0.3989422804014327
            back[r, :, col] = (gv * slope).astype(bf)
            return carry

        lax.fori_loop(0, pieces, tile, 0)

        @pl.when(r + 3 < experts)
        def _():
            for h in range(2):
                z_copy(r + 2, h).wait_send()
                z_copy(r + 3, h).start()

        out = jnp.dot(hid[r], v_ref[...], preferred_element_type=f32)
        part[r, :, 0] = out.astype(bf).reshape(SPLIT, cap, width)
        r1_copy(r, 0).start()
        inn = lax.dot_general(
            back[r], u_ref[...], (((1,), (1,)), ((), ())), preferred_element_type=f32)
        part[r, :, 1] = inn.astype(bf).reshape(SPLIT, cap, width)
        r1_copy(r, 1).start()
        return carry

    lax.fori_loop(0, experts, step, 0)
    def ug_copy(n):
        col = pl.ds(pl.multiple_of(n * TILE, TILE), TILE)
        return pltpu.make_async_copy(ug.at[:, col], ug_hbm.at[0, :, col], g_sem.at[0, n])

    def dg_copy(n):
        col = pl.ds(pl.multiple_of(n * TILE, TILE), TILE)
        return pltpu.make_async_copy(dg.at[col, :], dg_hbm.at[0, col, :], g_sem.at[1, n])

    total = experts * SPLIT * cap

    def grads(n, carry):
        @pl.when(n == 1)
        def _():
            pair_sum(experts - 1)
            for h in range(2):
                quad_sum(experts - 2, h)

        @pl.when(n == pieces - 1)
        def _():
            quad_sum(experts - 1, 0)

        col = pl.ds(pl.multiple_of(n * TILE, TILE), TILE)
        x = rows[:, :, 0].reshape(total, width)
        b = back[:, :, col].reshape(total, TILE)
        ug[:, col] = lax.dot_general(
            x, b, (((0,), (0,)), ((), ())), preferred_element_type=f32).astype(bf)
        ug_copy(n).start()
        g = rows[:, :, 1].reshape(total, width)
        h = hid[:, :, col].reshape(total, TILE)
        dg[col, :] = lax.dot_general(
            h, g, (((0,), (0,)), ((), ())), preferred_element_type=f32).astype(bf)
        dg_copy(n).start()
        return carry

    lax.fori_loop(0, pieces, grads, 0)
    quad_sum(experts - 1, 1)

    layer = jnp.zeros((tok, width), f32)
    grad = jnp.zeros((tok, width), f32)
    for r in range(experts):
        if r:
            r3_copy(r, 0).wait_recv()
        block = ret.at[r] if r else part.at[0, 0]
        pick = jnp.where(choose(r), 1.0, 0.0).astype(bf)
        picked = lax.dot_general(
            pick, block[0], (((0,), (0,)), ((), ())), preferred_element_type=f32)
        layer = layer + picked * gate_col[:, r:r + 1]
        if r:
            r3_copy(r, 1).wait_recv()
        grad = grad + lax.dot_general(
            pick, block[1], (((0,), (0,)), ((), ())), preferred_element_type=f32)
    lo_ref[...] = layer.astype(bf)
    tg_ref[...] = grad.astype(bf)

    def drain(r, carry):
        for h in range(2):
            y_copy(r, h).wait_send()
            c_copy(r, h).wait_send()
            f_copy(r, h).wait_send()
            r1_copy(r, h).wait_send()
            r2_copy(r, h).wait_send()

            @pl.when(r >= 1)
            def _():
                r3_copy(r, h).wait_send()

        return carry

    lax.fori_loop(0, experts, drain, 0)
    for h in range(2):
        z_copy(experts - 1, h).wait_send()

    def drain_grads(n, carry):
        ug_copy(n).wait()
        dg_copy(n).wait()
        return carry

    lax.fori_loop(0, pieces, drain_grads, 0)


def local(tokens, routes, gate_weights, image_counts, cotangent, up_weight, down_weight):
    shards = lax.axis_size("expert")
    experts = shards // SPLIT
    tok, width = tokens.shape
    hidden = up_weight.shape[2]
    capacity = SPLIT * ((10 * tok + 4 * SPLIT * experts - 1) // (4 * SPLIT * experts))
    cap = -(-capacity // 16) * 16
    bf = jnp.bfloat16
    vmem = pl.BlockSpec(memory_space=pltpu.VMEM)
    smem = pl.BlockSpec(memory_space=pltpu.SMEM)
    hbm = pl.BlockSpec(memory_space=pl.ANY)
    rows = experts * SPLIT * cap
    return pl.pallas_call(
        functools.partial(kernel, experts),
        out_shape=(
            jax.ShapeDtypeStruct((tok, width), bf),
            jax.ShapeDtypeStruct((tok, width), bf),
            jax.ShapeDtypeStruct((1, width, hidden), bf),
            jax.ShapeDtypeStruct((1, hidden, width), bf),
        ),
        in_specs=[vmem, vmem, smem, vmem, vmem, hbm, hbm],
        out_specs=(vmem, vmem, hbm, hbm),
        scratch_shapes=[
            pltpu.VMEM((width, hidden), bf),
            pltpu.VMEM((hidden, width), bf),
            pltpu.VMEM((experts, 2, cap, width), bf),
            pltpu.VMEM((experts, SPLIT, 2, cap, width), bf),
            pltpu.VMEM((experts, SPLIT, 2, cap, width), bf),
            pltpu.VMEM((experts, 2, 2, cap, width), bf),
            pltpu.VMEM((experts, 2, cap, width), bf),
            pltpu.VMEM((experts, 2, cap, width), bf),
            pltpu.VMEM((experts, SPLIT * cap, hidden), bf),
            pltpu.VMEM((experts, SPLIT * cap, hidden), bf),
            pltpu.VMEM((width, hidden), bf),
            pltpu.VMEM((hidden, width), bf),
            pltpu.SemaphoreType.DMA((7, experts, 2)),
            pltpu.SemaphoreType.DMA((7, experts, 2)),
            pltpu.SemaphoreType.DMA((2,)),
            pltpu.SemaphoreType.DMA((2, hidden // TILE)),
        ],
        compiler_params=pltpu.CompilerParams(
            collective_id=0, has_side_effects=True, vmem_limit_bytes=58 * 1024 * 1024
        ),
        cost_estimate=pl.CostEstimate(
            flops=12 * rows * width * hidden,
            bytes_accessed=8 * width * hidden,
            transcendentals=2 * rows * hidden,
        ),
    )(routes.T, gate_weights.T, image_counts, tokens, cotangent, up_weight, down_weight)


def solution(mesh):
    placed = (
        P(("groups", "expert"), None),
        P(("groups", "expert"), None),
        P(("groups", "expert"), None),
        P(("groups", "expert"), None),
        P(("groups", "expert"), None),
        P("expert", None, None),
        P("expert", None, None),
    )
    return jax.shard_map(
        local,
        mesh=mesh,
        in_specs=placed,
        out_specs=(
            P(("groups", "expert"), None),
            P(("groups", "expert"), None),
            P(("groups", "expert"), None, None),
            P(("groups", "expert"), None, None),
        ),
        check_vma=False,
    )
```

```python
import functools

import jax
import jax.numpy as jnp
from jax import lax
from jax.experimental import pallas as pl
from jax.experimental.pallas import tpu as pltpu
from jax.sharding import PartitionSpec as P

SPLIT = 4
TILE = 256
Z, Y, C, F, R1, R2, R3 = range(7)


def kernel(
    experts, rt_ref, gt_ref, cnt_ref, tok_ref, cot_ref, u_hbm, v_hbm,
    lo_ref, tg_ref, ug_hbm, dg_hbm,
    u_ref, v_ref, send, rows, part, t1, t2, ret, hid, back, ug, dg,
    send_sem, recv_sem, w_sem, g_sem,
):
    me = lax.axis_index("expert")
    mine = me // SPLIT
    quarter = lax.rem(me, SPLIT)
    far = mine * SPLIT + lax.rem(quarter + 2, SPLIT)
    near = me + 1 - 2 * lax.rem(me, 2)
    tok, width = tok_ref.shape
    cap = send.shape[2]
    hidden = u_ref.shape[1]
    pieces = hidden // TILE
    bf, f32 = jnp.bfloat16, jnp.float32

    def turn(r):
        half = (r + 1) // 2
        return half if r % 2 else experts - half

    def turn_of(r):
        if isinstance(r, int):
            return turn(r)
        half = (r + 1) // 2
        return jnp.where(lax.rem(r, 2) == 1, half, experts - half)

    def dest(r):
        return lax.rem(mine - turn_of(r) + experts, experts)

    def source(r):
        return lax.rem(mine + turn_of(r), experts)

    def copy(src, dst, kind, r, h, dev):
        return pltpu.make_async_remote_copy(
            src_ref=src, dst_ref=dst,
            send_sem=send_sem.at[kind, r, h], recv_sem=recv_sem.at[kind, r, h],
            device_id={"expert": dev}, device_id_type=pl.DeviceIdType.MESH,
        )

    def z_copy(r, h):
        return copy(send.at[r, h], rows.at[r, 0, h], Z, r, h, dest(r) * SPLIT + quarter)

    def y_copy(r, h):
        return copy(rows.at[r, 0, h], rows.at[r, 1, h], Y, r, h, far)

    def c_copy(r, h):
        return copy(rows.at[r, 0, h], rows.at[r, 2, h], C, r, h, near)

    def f_copy(r, h):
        return copy(rows.at[r, 1, h], rows.at[r, 3, h], F, r, h, near)

    def r1_copy(r, h):
        return copy(part.at[r, pl.ds(2, 2), h], t1.at[r, :, h], R1, r, h, near)

    def r2_copy(r, h):
        return copy(part.at[r, 1, h], t2.at[r, h], R2, r, h, far)

    def r3_copy(r, h):
        return copy(part.at[r, 0, h], ret.at[r, h], R3, r, h, source(r) * SPLIT + quarter)

    u_copy = pltpu.make_async_copy(u_hbm.at[0], u_ref, w_sem.at[0])
    v_copy = pltpu.make_async_copy(v_hbm.at[0], v_ref, w_sem.at[1])
    u_copy.start()
    v_copy.start()

    barrier = pltpu.get_barrier_semaphore()
    for r in range(1, experts):
        pl.semaphore_signal(
            barrier, inc=1, device_id={"expert": dest(r) * SPLIT + quarter},
            device_id_type=pl.DeviceIdType.MESH,
        )
    for other in (far, near):
        pl.semaphore_signal(
            barrier, inc=1, device_id={"expert": other}, device_id_type=pl.DeviceIdType.MESH
        )

    heads = max(8, experts)
    row_id = lax.broadcasted_iota(jnp.int32, (heads, tok), 0)
    expert_id = lax.rem(mine - turn_of(row_id) + heads * experts, experts)
    r0 = jnp.broadcast_to(rt_ref[0:1, :], (heads, tok))
    r1 = jnp.broadcast_to(rt_ref[1:2, :], (heads, tok))
    g0 = jnp.broadcast_to(gt_ref[0:1, :], (heads, tok))
    g1 = jnp.broadcast_to(gt_ref[1:2, :], (heads, tok))
    takes0, takes1 = r0 == expert_id, r1 == expert_id
    member = jnp.where(takes0, 1.0, jnp.where(takes1, 1.0, 0.0))
    gate = jnp.where(takes0, g0, jnp.where(takes1, g1, 0.0))
    earlier = jnp.where(
        lax.broadcasted_iota(jnp.int32, (tok, tok), 0)
        < lax.broadcasted_iota(jnp.int32, (tok, tok), 1), 1.0, 0.0)
    rank = jnp.dot(member.astype(bf), earlier.astype(bf), preferred_element_type=f32)
    rank = jnp.where(member > 0.5, rank, -1.0)
    images = cnt_ref.shape[1]
    position = lax.broadcasted_iota(jnp.int32, (heads, tok), 1)
    own = jnp.ones((heads, tok), jnp.int32)
    start = jnp.int32(0)
    for j in range(images):
        count = cnt_ref[0, j]
        own = jnp.where(position >= start, count, own)
        start = start + count
    weight = gate * ((tok / images) / own.astype(f32))
    gate_col = jnp.transpose(gate)
    slot_id = lax.broadcasted_iota(jnp.int32, (cap, tok), 0).astype(f32)

    def choose(r):
        return slot_id == jnp.broadcast_to(rank[r:r + 1], (cap, tok))

    def fill(r, dst, send_half):
        hit = choose(r)
        pick = jnp.where(hit, 1.0, 0.0).astype(bf)
        dst[0] = jnp.dot(pick, tok_ref[...], preferred_element_type=f32).astype(bf)
        send_half(0)
        w = jnp.sum(
            jnp.where(hit, jnp.broadcast_to(weight[r:r + 1], (cap, tok)), 0.0),
            axis=1, keepdims=True)
        dst[1] = (jnp.dot(pick, cot_ref[...], preferred_element_type=f32) * w).astype(bf)
        send_half(1)

    def send_own(h):
        y_copy(0, h).start()
        c_copy(0, h).start()

    def send_first(h):
        if h == 0:
            pl.semaphore_wait(barrier, experts + 1)
        z_copy(1, h).start()

    fill(1, send.at[1], send_first)
    fill(0, rows.at[0, 0], send_own)
    for r in range(2, experts):
        fill(r, send.at[r], lambda h: None)
    for h in range(2):
        z_copy(1, h).wait_send()
        z_copy(2, h).start()
    u_copy.wait()
    v_copy.wait()

    def pair_sum(r):
        for h in range(2):
            r1_copy(r, h).wait_recv()
            for j in (1, 0):
                part[r, j, h] = (part[r, j, h].astype(f32) + t1[r, j, h].astype(f32)).astype(bf)
                if j == 1:
                    r2_copy(r, h).start()

    def quad_sum(r, h):
        r2_copy(r, h).wait_recv()
        part[r, 0, h] = (part[r, 0, h].astype(f32) + t2[r, h].astype(f32)).astype(bf)

        @pl.when(jnp.int32(r) >= 1)
        def _():
            r3_copy(r, h).start()

    def step(r, carry):
        for h in range(2):
            y_copy(r, h).wait_recv()
            f_copy(r, h).start()

        @pl.when(r >= 2)
        def _():
            pair_sum(r - 1)

        @pl.when(r + 1 < experts)
        def _():
            for h in range(2):
                z_copy(r + 1, h).wait_recv()
                y_copy(r + 1, h).start()
                c_copy(r + 1, h).start()

        @pl.when(r == 1)
        def _():
            pair_sum(0)

        @pl.when(r >= 2)
        def _():
            for h in range(2):
                quad_sum(r - 2, h)

        for h in range(2):
            c_copy(r, h).wait_recv()
            f_copy(r, h).wait_recv()

        def tile(n, carry):
            col = pl.ds(pl.multiple_of(n * TILE, TILE), TILE)
            x = rows[r, :, 0].reshape(SPLIT * cap, width)
            g = rows[r, :, 1].reshape(SPLIT * cap, width)
            pre = jnp.dot(x, u_ref[:, col], preferred_element_type=f32)
            gv = lax.dot_general(
                g, v_ref[col, :], (((1,), (1,)), ((), ())), preferred_element_type=f32)
            phi = 0.5 * (1.0 + lax.erf(pre * 0.7071067811865476))
            hid[r, :, col] = (pre * phi).astype(bf)
            slope = phi + pre * jnp.exp(-0.5 * pre * pre) * 0.3989422804014327
            back[r, :, col] = (gv * slope).astype(bf)
            return carry

        lax.fori_loop(0, pieces, tile, 0)

        @pl.when(r + 3 < experts)
        def _():
            for h in range(2):
                z_copy(r + 2, h).wait_send()
                z_copy(r + 3, h).start()

        out = jnp.dot(hid[r], v_ref[...], preferred_element_type=f32)
        part[r, :, 0] = out.astype(bf).reshape(SPLIT, cap, width)
        r1_copy(r, 0).start()
        inn = lax.dot_general(
            back[r], u_ref[...], (((1,), (1,)), ((), ())), preferred_element_type=f32)
        part[r, :, 1] = inn.astype(bf).reshape(SPLIT, cap, width)
        r1_copy(r, 1).start()
        return carry

    lax.fori_loop(0, experts, step, 0)
    def ug_copy(n):
        col = pl.ds(pl.multiple_of(n * TILE, TILE), TILE)
        return pltpu.make_async_copy(ug.at[:, col], ug_hbm.at[0, :, col], g_sem.at[0, n])

    def dg_copy(n):
        col = pl.ds(pl.multiple_of(n * TILE, TILE), TILE)
        return pltpu.make_async_copy(dg.at[col, :], dg_hbm.at[0, col, :], g_sem.at[1, n])

    total = experts * SPLIT * cap

    def grads(n, carry):
        @pl.when(n == 1)
        def _():
            pair_sum(experts - 1)
            for h in range(2):
                quad_sum(experts - 2, h)

        @pl.when(n == pieces - 1)
        def _():
            quad_sum(experts - 1, 0)

        col = pl.ds(pl.multiple_of(n * TILE, TILE), TILE)
        x = rows[:, :, 0].reshape(total, width)
        b = back[:, :, col].reshape(total, TILE)
        ug[:, col] = lax.dot_general(
            x, b, (((0,), (0,)), ((), ())), preferred_element_type=f32).astype(bf)
        ug_copy(n).start()
        g = rows[:, :, 1].reshape(total, width)
        h = hid[:, :, col].reshape(total, TILE)
        dg[col, :] = lax.dot_general(
            h, g, (((0,), (0,)), ((), ())), preferred_element_type=f32).astype(bf)
        dg_copy(n).start()
        return carry

    lax.fori_loop(0, pieces, grads, 0)
    quad_sum(experts - 1, 1)

    layer = jnp.zeros((tok, width), f32)
    grad = jnp.zeros((tok, width), f32)
    for r in range(experts):
        if r:
            r3_copy(r, 0).wait_recv()
        block = ret.at[r] if r else part.at[0, 0]
        pick = jnp.where(choose(r), 1.0, 0.0).astype(bf)
        picked = lax.dot_general(
            pick, block[0], (((0,), (0,)), ((), ())), preferred_element_type=f32)
        layer = layer + picked * gate_col[:, r:r + 1]
        if r:
            r3_copy(r, 1).wait_recv()
        grad = grad + lax.dot_general(
            pick, block[1], (((0,), (0,)), ((), ())), preferred_element_type=f32)
    lo_ref[...] = layer.astype(bf)
    tg_ref[...] = grad.astype(bf)

    def drain(r, carry):
        for h in range(2):
            y_copy(r, h).wait_send()
            c_copy(r, h).wait_send()
            f_copy(r, h).wait_send()
            r1_copy(r, h).wait_send()
            r2_copy(r, h).wait_send()

            @pl.when(r >= 1)
            def _():
                r3_copy(r, h).wait_send()

        return carry

    lax.fori_loop(0, experts, drain, 0)
    for h in range(2):
        z_copy(experts - 1, h).wait_send()

    def drain_grads(n, carry):
        ug_copy(n).wait()
        dg_copy(n).wait()
        return carry

    lax.fori_loop(0, pieces, drain_grads, 0)


def local(tokens, routes, gate_weights, image_counts, cotangent, up_weight, down_weight):
    shards = lax.axis_size("expert")
    experts = shards // SPLIT
    tok, width = tokens.shape
    hidden = up_weight.shape[2]
    capacity = SPLIT * ((10 * tok + 4 * SPLIT * experts - 1) // (4 * SPLIT * experts))
    cap = -(-capacity // 16) * 16
    bf = jnp.bfloat16
    vmem = pl.BlockSpec(memory_space=pltpu.VMEM)
    smem = pl.BlockSpec(memory_space=pltpu.SMEM)
    hbm = pl.BlockSpec(memory_space=pl.ANY)
    rows = experts * SPLIT * cap
    return pl.pallas_call(
        functools.partial(kernel, experts),
        out_shape=(
            jax.ShapeDtypeStruct((tok, width), bf),
            jax.ShapeDtypeStruct((tok, width), bf),
            jax.ShapeDtypeStruct((1, width, hidden), bf),
            jax.ShapeDtypeStruct((1, hidden, width), bf),
        ),
        in_specs=[vmem, vmem, smem, vmem, vmem, hbm, hbm],
        out_specs=(vmem, vmem, hbm, hbm),
        scratch_shapes=[
            pltpu.VMEM((width, hidden), bf),
            pltpu.VMEM((hidden, width), bf),
            pltpu.VMEM((experts, 2, cap, width), bf),
            pltpu.VMEM((experts, SPLIT, 2, cap, width), bf),
            pltpu.VMEM((experts, SPLIT, 2, cap, width), bf),
            pltpu.VMEM((experts, 2, 2, cap, width), bf),
            pltpu.VMEM((experts, 2, cap, width), bf),
            pltpu.VMEM((experts, 2, cap, width), bf),
            pltpu.VMEM((experts, SPLIT * cap, hidden), bf),
            pltpu.VMEM((experts, SPLIT * cap, hidden), bf),
            pltpu.VMEM((width, hidden), bf),
            pltpu.VMEM((hidden, width), bf),
            pltpu.SemaphoreType.DMA((7, experts, 2)),
            pltpu.SemaphoreType.DMA((7, experts, 2)),
            pltpu.SemaphoreType.DMA((2,)),
            pltpu.SemaphoreType.DMA((2, hidden // TILE)),
        ],
        compiler_params=pltpu.CompilerParams(
            collective_id=0, has_side_effects=True, vmem_limit_bytes=58 * 1024 * 1024
        ),
        cost_estimate=pl.CostEstimate(
            flops=12 * rows * width * hidden,
            bytes_accessed=8 * width * hidden,
            transcendentals=2 * rows * hidden,
        ),
    )(routes.T, gate_weights.T, image_counts, tokens, cotangent, up_weight, down_weight)


def solution(mesh):
    placed = (
        P(("groups", "expert"), None),
        P(("groups", "expert"), None),
        P(("groups", "expert"), None),
        P(("groups", "expert"), None),
        P(("groups", "expert"), None),
        P("expert", None, None),
        P("expert", None, None),
    )
    return jax.shard_map(
        local,
        mesh=mesh,
        in_specs=placed,
        out_specs=(
            P(("groups", "expert"), None),
            P(("groups", "expert"), None),
            P(("groups", "expert"), None, None),
            P(("groups", "expert"), None, None),
        ),
        check_vma=False,
    )
```
